512 devices in a mesh: dp: 4 (over x_lo, core), neg: 128 (over x_hi, y, z).
Axes of the slice: x: 4 (x_hi: 2, x_lo: 2; x = x_hi * 2 + x_lo), y: 4, z: 16, core: 2. Of those that a mesh axis runs over, the one named last changes fastest.
Arguments:
- queries: bfloat16 [262144, 1024], P(('dp', 'neg')), parts along dimension 0, may hold values from -48 to 48
- passages: bfloat16 [262144, 1024], P(('dp', 'neg')), parts along dimension 0, may hold values from -8 to 8
- partners: int32 [2, 128], replicated, may hold values from 0 to 127, as said below
- positives: int32 [262144], P(('dp', 'neg')), parts along dimension 0, may hold values from 0 to 511
Outputs:
- row_loss: float32 [262144], P(('dp', 'neg')), parts along dimension 0
- grad_queries: bfloat16 [262144, 1024], P(('dp', 'neg')), parts along dimension 0
- grad_passages: bfloat16 [262144, 1024], P(('dp', 'neg')), parts along dimension 0
The draws below stay inside these ranges and needn't reach their ends.
There are 4 independent parts, one for each index of `dp`. The reference program is written for one: setup_inputs(seed, part) draws one part's arguments, and reference() takes and returns one part's arrays. A program takes and returns all parts, laid end to end along the dimension named above; an argument that names none is the same for every part. Nothing has to cross between parts.
Inputs may be any that keep to these rules, and one draw needn't show every extreme that they name: `partners`: in each round r the table maps block b to b XOR 2**k_r, with a different k_r in each round, so each round pairs the blocks; one of the rounds pairs b with b XOR 128/2.
All inputs are finite; a program needn't handle non-finite values.
Results may differ from the reference program's by a relative error of at most 0.0034.
Values may be sent and summed in bfloat16 or wider, within the bound.
A program may use at most 64 MiB of HBM per device.

```python
import jax
import jax.numpy as jnp
from jax import lax

D = 1024
ROWS_DEV = 512
ROUNDS = 2
TOKENS = 65536
N_NEG = 128


def shared_rows(key):
    base = jnp.clip(jax.random.normal(jax.random.fold_in(key, 11), (TOKENS, D), jnp.float32), -6.0, 6.0)
    return base


def draw_passages(key, part):
    base = shared_rows(key)
    result = base
    return result.astype(jnp.bfloat16)


def draw_queries(key, part):
    key = jax.random.fold_in(key, 2)
    result = jnp.clip(jax.random.normal(key, (TOKENS, D), jnp.float32), -6.0, 6.0)
    return result.astype(jnp.bfloat16)


def draw_partners(key, part):
    key = jax.random.fold_in(key, 5)
    levels = N_NEG.bit_length() - 1
    lower = jax.random.permutation(jax.random.fold_in(key, 1), levels - 1).astype(jnp.int32)
    place = jax.random.randint(jax.random.fold_in(key, 2), (), 0, ROUNDS).astype(jnp.int32)
    steps = jnp.arange(ROUNDS, dtype=jnp.int32)
    source = jnp.clip(steps - (steps > place).astype(jnp.int32), 0, levels - 2)
    order = jnp.where(steps == place, jnp.int32(levels - 1), lower[source]).astype(jnp.int32)
    blocks = jnp.arange(N_NEG, dtype=jnp.int32)
    return jnp.bitwise_xor(blocks[None, :], jnp.left_shift(jnp.int32(1), order)[:, None])


def touch_ends(array, own_key, low, high):
    dims = array.shape
    spot = [jax.random.randint(jax.random.fold_in(own_key, axis), (), 0, dims[axis]) for axis in range(len(dims))]
    array = array.at[tuple(spot)].set(low)
    longest = dims.index(max(dims))
    spot[longest] = (spot[longest] + 1) % dims[longest]
    return array.at[tuple(spot)].set(high)


def setup_inputs(seed: int = 0, part: int = 0) -> dict:
    seeds = jax.random.split(jax.random.key(seed), 5)
    part_splits = jax.random.split(jax.random.fold_in(seeds[4], part), 5)
    return {
        "queries": draw_queries(jax.random.fold_in(jax.random.fold_in(seeds[4], part), 71), part),
        "passages": draw_passages(jax.random.fold_in(jax.random.fold_in(seeds[4], part), 71), part),
        "partners": draw_partners(jax.random.fold_in(seeds[4], 71), part),
        "positives": touch_ends(jax.random.randint(part_splits[3], (TOKENS,), 0, ROWS_DEV), jax.random.fold_in(part_splits[3], 1), 0, ROWS_DEV - 1).astype(jnp.int32),
    }


def tile_scores(left, right, scale):
    return lax.dot_general(left, right, (((1,), (1,)), ((), ())), preferred_element_type=jnp.float32) * scale


def tile_back(weights, rows):
    return lax.dot_general(weights, rows, (((0,), (0,)), ((), ())), preferred_element_type=jnp.float32)


def reference(queries, passages, partners, positives):
    query_blocks = queries.reshape(N_NEG, ROWS_DEV, D)
    passage_blocks = passages.reshape(N_NEG, ROWS_DEV, D)
    positive_blocks = positives.reshape(N_NEG, ROWS_DEV)
    scale = D ** -0.5
    columns = jnp.arange(ROWS_DEV, dtype=jnp.int32)

    def one_block(index):
        query = query_blocks[index]
        blocks = [passage_blocks[index]] + [passage_blocks[partners[r, index]] for r in range(ROUNDS)]
        scores = [tile_scores(query, block, scale) for block in blocks]
        top = scores[0].max(axis=1)
        for tile in scores[1:]:
            top = jnp.maximum(top, tile.max(axis=1))
        total = jnp.zeros_like(top)
        for tile in scores:
            total = total + jnp.sum(jnp.exp(tile - top[:, None]), axis=1)
        lse = top + jnp.log(total)
        hit = positive_blocks[index][:, None] == columns[None, :]
        loss = lse - jnp.sum(jnp.where(hit, scores[0], 0.0), axis=1)
        weights = []
        for k, tile in enumerate(scores):
            prob = jnp.exp(tile - lse[:, None])
            if k == 0:
                prob = prob - hit.astype(jnp.float32)
            weights.append(prob.astype(jnp.bfloat16))
        grad_query = jnp.zeros((ROWS_DEV, D), jnp.float32)
        for wtile, block in zip(weights, blocks):
            grad_query = grad_query + jnp.dot(wtile, block, preferred_element_type=jnp.float32)
        own = tile_back(weights[0], query)
        sent = jnp.stack([tile_back(w, query).astype(jnp.bfloat16) for w in weights[1:]])
        return loss, grad_query.astype(jnp.bfloat16), own, sent

    loss, grad_query, own, sent = lax.map(one_block, jnp.arange(N_NEG, dtype=jnp.int32))
    total = own
    for r in range(ROUNDS):
        total = total + sent[partners[r], r].astype(jnp.float32)
    return loss.reshape(TOKENS), grad_query.reshape(TOKENS, D), total.astype(jnp.bfloat16).reshape(TOKENS, D)
```

```python
import functools

import jax
import jax.numpy as jnp
from jax import lax
from jax.experimental import pallas as pl
from jax.experimental.pallas import tpu as pltpu
from jax.sharding import PartitionSpec as P

MESH = pl.DeviceIdType.MESH
CHUNK = 128
EARLY = 2


def nt(left, right):
    return lax.dot_general(left, right, (((1,), (1,)), ((), ())), preferred_element_type=jnp.float32)


def tn(left, right):
    return lax.dot_general(left, right, (((0,), (0,)), ((), ())), preferred_element_type=jnp.float32)


def nn(left, right):
    return jnp.dot(left, right, preferred_element_type=jnp.float32)


def kernel(strides, scale, q_hbm, p_hbm, pos_ref, loss_ref, dq_hbm, dp_hbm,
           q, p, pin, qin, s, w, own, part, outq, outp, lse_own, lse_in,
           load_sem, store_sem, p_send, p_recv, q_send, q_recv, l_send, l_recv):
    rows, width = q.shape
    n = rows // CHUNK
    dp, me = lax.axis_index("dp"), lax.axis_index("neg")
    peers = [(dp, jnp.bitwise_xor(me, stride)) for stride in strides]

    loads = [pltpu.make_async_copy(p_hbm, p, load_sem.at[0]), pltpu.make_async_copy(q_hbm, q, load_sem.at[1])]
    for load in loads:
        load.start()
    barrier = pltpu.get_barrier_semaphore()
    for peer in peers:
        pl.semaphore_signal(barrier, inc=1, device_id=peer, device_id_type=MESH)
    pl.semaphore_wait(barrier, len(peers))

    def part_of(c):
        return pl.ds(pl.multiple_of(c * CHUNK, CHUNK), CHUNK)

    def send(src, dst, send_sem, recv_sem, i, c):
        return pltpu.make_async_remote_copy(
            src_ref=src.at[part_of(c)], dst_ref=dst.at[i, part_of(c)],
            send_sem=send_sem.at[i, c], recv_sem=recv_sem.at[i, c],
            device_id=peers[i], device_id_type=MESH)

    def send_p(i, c):
        return send(p_hbm, pin, p_send, p_recv, i, c)

    def send_q(i, c):
        return send(q_hbm, qin, q_send, q_recv, i, c)

    def send_lse(i):
        return pltpu.make_async_remote_copy(
            src_ref=lse_own, dst_ref=lse_in.at[i], send_sem=l_send.at[i], recv_sem=l_recv.at[i],
            device_id=peers[i], device_id_type=MESH)

    for c in range(n):
        for i in (0, 1):
            send_p(i, c).start()
    for c in range(EARLY):
        for i in (0, 1):
            send_q(i, c).start()

    for load in loads:
        load.wait()

    def scores(k, block, c, top):
        tile = nt(block, q[...]) * scale
        s[k, part_of(c)] = tile
        return jnp.maximum(top, jnp.max(tile.reshape(CHUNK // 8, 8, rows), axis=0))

    def own_scores(c, top):
        return scores(0, p[part_of(c)], c, top)

    top = lax.fori_loop(0, n, own_scores, jnp.full((8, rows), -jnp.inf, jnp.float32))

    def partner_scores(c, top):
        for i in (0, 1):
            send_p(i, c).wait_recv()
            top = scores(i + 1, pin[i, part_of(c)], c, top)
        return top

    top = lax.fori_loop(0, n, partner_scores, top)
    top = jnp.max(top, axis=0, keepdims=True)

    def add_up(c, total):
        for k in range(3):
            tile = jnp.exp(s[k, part_of(c)] - top)
            total = total + jnp.sum(tile.reshape(CHUNK // 8, 8, rows), axis=0)
        return total

    total = lax.fori_loop(0, n, add_up, jnp.zeros((8, rows), jnp.float32))
    lse = top + jnp.log(jnp.sum(total, axis=0, keepdims=True))
    lse_own[...] = jnp.broadcast_to(lse, lse_own.shape)
    for i in (0, 1):
        send_lse(i).start()
    for c in range(EARLY, n):
        for i in (0, 1):
            send_q(i, c).start()

    positive = pos_ref[...]

    def weigh(c, picked):
        tile = s[0, part_of(c)]
        hit = lax.broadcasted_iota(jnp.int32, tile.shape, 0) + c * CHUNK == positive
        picked = picked + jnp.sum(jnp.where(hit, tile, 0.0).reshape(CHUNK // 8, 8, rows), axis=0)
        w[0, part_of(c)] = (jnp.exp(tile - lse) - hit.astype(jnp.float32)).astype(jnp.bfloat16)
        for k in (1, 2):
            w[k, part_of(c)] = jnp.exp(s[k, part_of(c)] - lse).astype(jnp.bfloat16)
        return picked

    picked = lax.fori_loop(0, n, weigh, jnp.zeros((8, rows), jnp.float32))
    loss_ref[...] = lse - jnp.sum(picked, axis=0, keepdims=True)

    def store(src, dst, sem, c):
        return pltpu.make_async_copy(src.at[part_of(c)], dst.at[part_of(c)], sem.at[c])

    def grad_q(c, _):
        grad = tn(w[0, :, part_of(c)], p[...])
        for i in (0, 1):
            grad = grad + tn(w[i + 1, :, part_of(c)], pin[i])
        outq[part_of(c)] = grad.astype(jnp.bfloat16)
        store(outq, dq_hbm, store_sem.at[0], c).start()
        own[part_of(c)] = nn(w[0, part_of(c)], q[...])
        return 0

    lax.fori_loop(0, n, grad_q, 0)
    for i in (0, 1):
        send_lse(i).wait_recv()

    def partner_weights(i, c):
        send_q(i, c).wait_recv()
        tile = nt(p[...], qin[i, part_of(c)]) * scale
        return jnp.exp(tile - lse_in[i, 0:1, part_of(c)]).astype(jnp.bfloat16)

    def partner_back(c, _):
        for i in (0, 1):
            term = nn(partner_weights(i, c), qin[i, part_of(c)])

            @pl.when(c == 0)
            def _():
                part[i] = term

            @pl.when(c > 0)
            def _():
                part[i] += term
        return 0

    lax.fori_loop(0, n - 1, partner_back, 0)
    last = n - 1
    part[0] += nn(partner_weights(0, last), qin[0, part_of(last)])
    own[...] += part[0].astype(jnp.bfloat16).astype(jnp.float32)
    w[0, :, 0:CHUNK] = partner_weights(1, last)

    def finish(c, _):
        mine = part[1, part_of(c)] + nn(w[0, part_of(c), 0:CHUNK], qin[1, part_of(last)])
        outp[part_of(c)] = (own[part_of(c)] + mine.astype(jnp.bfloat16).astype(jnp.float32)).astype(jnp.bfloat16)
        store(outp, dp_hbm, store_sem.at[1], c).start()
        return 0

    lax.fori_loop(0, n, finish, 0)
    for c in range(n):
        for i in (0, 1):
            send_p(i, c).wait_send()
            send_q(i, c).wait_send()
    for i in (0, 1):
        send_lse(i).wait_send()
    for c in range(n):
        store(outq, dq_hbm, store_sem.at[0], c).wait()
        store(outp, dp_hbm, store_sem.at[1], c).wait()


def call(level, half, scale, queries, passages, positives):
    rows, width = queries.shape
    n = rows // CHUNK
    flops = 11 * 2 * rows * rows * width
    vmem, dma = pltpu.VMEM, pltpu.SemaphoreType.DMA
    anywhere = pl.BlockSpec(memory_space=pl.ANY)
    inside = pl.BlockSpec(memory_space=pltpu.VMEM)
    return pl.pallas_call(
        functools.partial(kernel, (half, 2**level), scale),
        out_shape=(
            jax.ShapeDtypeStruct((1, rows), jnp.float32),
            jax.ShapeDtypeStruct((rows, width), jnp.bfloat16),
            jax.ShapeDtypeStruct((rows, width), jnp.bfloat16),
        ),
        in_specs=[anywhere, anywhere, inside],
        out_specs=(inside, anywhere, anywhere),
        scratch_shapes=[
            vmem((rows, width), jnp.bfloat16),
            vmem((rows, width), jnp.bfloat16),
            vmem((2, rows, width), jnp.bfloat16),
            vmem((2, rows, width), jnp.bfloat16),
            vmem((3, rows, rows), jnp.float32),
            vmem((3, rows, rows), jnp.bfloat16),
            vmem((rows, width), jnp.float32),
            vmem((2, rows, width), jnp.float32),
            vmem((rows, width), jnp.bfloat16),
            vmem((rows, width), jnp.bfloat16),
            vmem((8, rows), jnp.float32),
            vmem((2, 8, rows), jnp.float32),
            dma((2,)),
            dma((2, n)),
            dma((2, n)),
            dma((2, n)),
            dma((2, n)),
            dma((2, n)),
            dma((2,)),
            dma((2,)),
        ],
        name=f"exchange_{level}",
        cost_estimate=pl.CostEstimate(flops=flops, bytes_accessed=8 * rows * width, transcendentals=8 * rows * rows),
        compiler_params=pltpu.CompilerParams(
            collective_id=level, has_side_effects=True, vmem_limit_bytes=48 * 2**20),
    )(queries, passages, positives)


def per_device(queries, passages, partners, positives):
    rows, width = queries.shape
    size = lax.axis_size("neg")
    half = size // 2
    other = partners[0, 0] ^ partners[1, 0] ^ half
    levels = half.bit_length() - 1
    index = sum((other >= 2**j).astype(jnp.int32) for j in range(1, levels))
    branches = [functools.partial(call, level, half, width ** (-0.5)) for level in range(levels)]
    loss, grad_queries, grad_passages = lax.switch(index, branches, queries, passages, positives.reshape(1, rows))
    return loss.reshape(rows), grad_queries, grad_passages


def solution(mesh):
    placed = (P(("dp", "neg"), None), P(("dp", "neg"), None), P(), P(("dp", "neg")))
    return jax.shard_map(
        per_device,
        mesh=mesh,
        in_specs=placed,
        out_specs=(P(("dp", "neg")), P(("dp", "neg"), None), P(("dp", "neg"), None)),
        check_vma=False,
    )
```

```python
import functools

import jax
import jax.numpy as jnp
from jax import lax
from jax.experimental import pallas as pl
from jax.experimental.pallas import tpu as pltpu
from jax.sharding import PartitionSpec as P

MESH = pl.DeviceIdType.MESH
CHUNK = 128
EARLY = 2


def nt(left, right):
    return lax.dot_general(left, right, (((1,), (1,)), ((), ())), preferred_element_type=jnp.float32)


def tn(left, right):
    return lax.dot_general(left, right, (((0,), (0,)), ((), ())), preferred_element_type=jnp.float32)


def nn(left, right):
    return jnp.dot(left, right, preferred_element_type=jnp.float32)


def exchange(strides, scale, q_hbm, p_hbm, pos_hbm, loss_ref, dq_ref, dp_ref,
             q, pos, allp, qin, s0, sp, w0, wp, own, part, w, lse_own, lse_in,
             load_sem, p_send, p_recv, q_send, q_recv, l_send, l_recv):
    rows, width = q.shape
    n = rows // CHUNK
    pair = 2 * CHUNK
    dp, me = lax.axis_index("dp"), lax.axis_index("neg")
    peers = [(dp, jnp.bitwise_xor(me, stride)) for stride in strides]

    loads = [
        pltpu.make_async_copy(p_hbm, allp.at[pl.ds(0, rows)], load_sem.at[0]),
        pltpu.make_async_copy(q_hbm, q, load_sem.at[1]),
        pltpu.make_async_copy(pos_hbm, pos, load_sem.at[2]),
    ]
    for load in loads:
        load.start()
    barrier = pltpu.get_barrier_semaphore()
    for peer in peers:
        pl.semaphore_signal(barrier, inc=1, device_id=peer, device_id_type=MESH)
    pl.semaphore_wait(barrier, len(peers))

    def chunk(c):
        return pl.ds(pl.multiple_of(c * CHUNK, CHUNK), CHUNK)

    def send_p(i, c):
        at = pl.multiple_of(rows + c * pair + i * CHUNK, CHUNK)
        return pltpu.make_async_remote_copy(
            src_ref=p_hbm.at[chunk(c)], dst_ref=allp.at[pl.ds(at, CHUNK)],
            send_sem=p_send.at[i, c], recv_sem=p_recv.at[i, c], device_id=peers[i], device_id_type=MESH)

    def send_q(i, c):
        return pltpu.make_async_remote_copy(
            src_ref=q_hbm.at[chunk(c)], dst_ref=qin.at[c, pl.ds(i * CHUNK, CHUNK)],
            send_sem=q_send.at[i, c], recv_sem=q_recv.at[i, c], device_id=peers[i], device_id_type=MESH)

    def send_lse(i):
        return pltpu.make_async_remote_copy(
            src_ref=lse_own, dst_ref=lse_in.at[i], send_sem=l_send.at[i], recv_sem=l_recv.at[i],
            device_id=peers[i], device_id_type=MESH)

    for c in range(n):
        for i in (0, 1):
            send_p(i, c).start()
    for c in range(EARLY):
        for i in (0, 1):
            send_q(i, c).start()
    for load in loads:
        load.wait()

    def fold(tile, combine):
        return combine(tile.reshape(tile.shape[0] // 8, 8, rows), axis=0)

    def own_scores(c, top):
        tile = nt(allp[chunk(c)], q[...]) * scale
        s0[chunk(c)] = tile
        return jnp.maximum(top, fold(tile, jnp.max))

    top = lax.fori_loop(0, n, own_scores, jnp.full((8, rows), -jnp.inf, jnp.float32))

    def partner_scores(c, top):
        for i in (0, 1):
            send_p(i, c).wait_recv()
        tile = nt(allp[pl.ds(pl.multiple_of(rows + c * pair, pair), pair)], q[...]) * scale
        sp[c] = tile
        return jnp.maximum(top, fold(tile, jnp.max))

    top = lax.fori_loop(0, n, partner_scores, top)
    top = jnp.max(top, axis=0, keepdims=True)

    def add_up(c, total):
        return total + fold(jnp.exp(s0[chunk(c)] - top), jnp.sum) + fold(jnp.exp(sp[c] - top), jnp.sum)

    total = lax.fori_loop(0, n, add_up, jnp.zeros((8, rows), jnp.float32))
    lse = top + jnp.log(jnp.sum(total, axis=0, keepdims=True))
    lse_own[...] = jnp.broadcast_to(lse, lse_own.shape)
    for i in (0, 1):
        send_lse(i).start()
    for c in range(EARLY, n):
        for i in (0, 1):
            send_q(i, c).start()

    positive = pos[...]

    def weigh(c, picked):
        tile = s0[chunk(c)]
        hit = lax.broadcasted_iota(jnp.int32, tile.shape, 0) + c * CHUNK == positive
        picked = picked + fold(jnp.where(hit, tile, 0.0), jnp.sum)
        w0[chunk(c)] = (jnp.exp(tile - lse) - hit.astype(jnp.float32)).astype(jnp.bfloat16)
        wp[pl.ds(pl.multiple_of(c * pair, pair), pair)] = jnp.exp(sp[c] - lse).astype(jnp.bfloat16)
        return picked

    picked = lax.fori_loop(0, n, weigh, jnp.zeros((8, rows), jnp.float32))
    loss_ref[...] = lse - jnp.sum(picked, axis=0, keepdims=True)

    def local_grads(c, _):
        grad = tn(w0[:, chunk(c)], allp[pl.ds(0, rows)]) + tn(wp[:, chunk(c)], allp[pl.ds(rows, 2 * rows)])
        dq_ref[chunk(c)] = grad.astype(jnp.bfloat16)
        own[chunk(c)] = nn(w0[chunk(c)], q[...])
        return 0

    lax.fori_loop(0, n, local_grads, 0)
    for i in (0, 1):
        send_lse(i).wait_recv()

    def partner_weights(c):
        for i in (0, 1):
            send_q(i, c).wait_recv()
        tile = nt(allp[pl.ds(0, rows)], qin[c]) * scale
        lses = jnp.concatenate([lse_in[i, 0:1, chunk(c)] for i in (0, 1)], axis=1)
        w[...] = jnp.exp(tile - lses).astype(jnp.bfloat16)

    halves = [pl.ds(i * CHUNK, CHUNK) for i in (0, 1)]

    def partner_back(c, first):
        partner_weights(c)

        def columns(j, _):
            span = pl.ds(pl.multiple_of(j * 256, 256), 256)
            for i in (0, 1):
                term = nn(w[:, halves[i]], qin[c, halves[i], span])
                part[i, :, span] = term if first else part[i, :, span] + term
            return 0

        lax.fori_loop(0, width // 256, columns, 0)

    partner_back(0, True)

    def more(c, _):
        partner_back(c, False)
        return 0

    lax.fori_loop(1, n - 1, more, 0)
    partner_weights(n - 1)

    def finish(c, _):
        big = pl.ds(pl.multiple_of(c * 256, 256), 256)
        total = own[big]
        for i in (0, 1):
            mine = part[i, big] + nn(w[big, halves[i]], qin[n - 1, halves[i]])
            total = total + mine.astype(jnp.bfloat16).astype(jnp.float32)
        dp_ref[big] = total.astype(jnp.bfloat16)
        return 0

    lax.fori_loop(0, 2, finish, 0)
    for c in range(n):
        for i in (0, 1):
            send_p(i, c).wait_send()
            send_q(i, c).wait_send()
    for i in (0, 1):
        send_lse(i).wait_send()


def call_exchange(level, half, scale, queries, passages, positives):
    rows, width = queries.shape
    n = rows // CHUNK
    vmem, dma = pltpu.VMEM, pltpu.SemaphoreType.DMA
    f32, bf16 = jnp.float32, jnp.bfloat16
    outside = pl.BlockSpec(memory_space=pltpu.HBM)
    inside = pl.BlockSpec(memory_space=pltpu.VMEM)
    return pl.pallas_call(
        functools.partial(exchange, (half, 2**level), scale),
        out_shape=(vmem((1, rows), f32), vmem((rows, width), bf16), vmem((rows, width), bf16)),
        in_specs=[outside] * 3,
        out_specs=(inside,) * 3,
        scratch_shapes=[
            vmem((rows, width), bf16),
            vmem((1, rows), jnp.int32),
            vmem((3 * rows, width), bf16),
            vmem((n, 2 * CHUNK, width), bf16),
            vmem((rows, rows), f32),
            vmem((n, 2 * CHUNK, rows), f32),
            vmem((rows, rows), bf16),
            vmem((2 * rows, rows), bf16),
            vmem((rows, width), f32),
            vmem((2, rows, width), f32),
            vmem((rows, 2 * CHUNK), bf16),
            vmem((8, rows), f32),
            vmem((2, 8, rows), f32),
            dma((3,)),
            dma((2, n)),
            dma((2, n)),
            dma((2, n)),
            dma((2, n)),
            dma((2,)),
            dma((2,)),
        ],
        name=f"exchange_{level}",
        cost_estimate=pl.CostEstimate(
            flops=22 * rows * rows * width, bytes_accessed=8 * rows * width, transcendentals=8 * rows * rows),
        compiler_params=pltpu.CompilerParams(
            collective_id=level, has_side_effects=True, vmem_limit_bytes=32 * 2**20),
    )(queries, passages, positives)


def write_out(loss, dq, dp, loss_hbm, dq_hbm, dp_hbm, sem):
    n = dq.shape[0] // CHUNK
    copies = [pltpu.make_async_copy(loss, loss_hbm, sem.at[2 * n])]
    for c in range(n):
        block = pl.ds(c * CHUNK, CHUNK)
        copies.append(pltpu.make_async_copy(dq.at[block], dq_hbm.at[block], sem.at[c]))
        copies.append(pltpu.make_async_copy(dp.at[block], dp_hbm.at[block], sem.at[n + c]))
    for copy in copies:
        copy.start()
    for copy in copies:
        copy.wait()


def call_write_out(*parts):
    outside = pl.BlockSpec(memory_space=pltpu.HBM)
    inside = pl.BlockSpec(memory_space=pltpu.VMEM)
    return pl.pallas_call(
        write_out,
        out_shape=tuple(jax.ShapeDtypeStruct(part.shape, part.dtype) for part in parts),
        in_specs=[inside] * 3,
        out_specs=(outside,) * 3,
        scratch_shapes=[pltpu.SemaphoreType.DMA((2 * (parts[1].shape[0] // CHUNK) + 1,))],
        name="write_out",
        compiler_params=pltpu.CompilerParams(vmem_limit_bytes=8 * 2**20),
    )(*parts)


def choose(half, levels, partners, index):
    other = partners[0, 0] ^ partners[1, 0] ^ half
    place = jnp.int32(0)
    for j in range(1, levels):
        place = place + (other >= 2**j).astype(jnp.int32)
    index[0] = place


def call_choose(half, levels, partners):
    return pl.pallas_call(
        functools.partial(choose, half, levels),
        out_shape=pltpu.SMEM((1,), jnp.int32),
        in_specs=[pl.BlockSpec(memory_space=pltpu.SMEM)],
        out_specs=pl.BlockSpec(memory_space=pltpu.SMEM),
        name="choose",
    )(partners)


def per_device(queries, passages, partners, positives):
    rows, width = queries.shape
    half = lax.axis_size("neg") // 2
    levels = half.bit_length() - 1
    index = call_choose(half, levels, partners)[0]
    branches = [functools.partial(call_exchange, level, half, width ** (-0.5)) for level in range(levels)]
    parts = lax.switch(index, branches, queries, passages, positives.reshape(1, rows))
    loss, grad_queries, grad_passages = call_write_out(*parts)
    return loss.reshape(rows), grad_queries, grad_passages


def solution(mesh):
    placed = (P(("dp", "neg"), None), P(("dp", "neg"), None), P(), P(("dp", "neg")))
    return jax.shard_map(
        per_device,
        mesh=mesh,
        in_specs=placed,
        out_specs=(P(("dp", "neg")), P(("dp", "neg"), None), P(("dp", "neg"), None)),
        check_vma=False,
    )
```

```python
import functools

import jax
import jax.numpy as jnp
from jax import lax
from jax.experimental import pallas as pl
from jax.experimental.pallas import tpu as pltpu
from jax.sharding import PartitionSpec as P

MESH = pl.DeviceIdType.MESH
TILE = 128
EARLY = 2
FIN = 256


def nt(left, right):
    return lax.dot_general(left, right, (((1,), (1,)), ((), ())), preferred_element_type=jnp.float32)


def tn(left, right):
    return lax.dot_general(left, right, (((0,), (0,)), ((), ())), preferred_element_type=jnp.float32)


def nn(left, right):
    return jnp.dot(left, right, preferred_element_type=jnp.float32)


def exchange(strides, scale, q_hbm, p_hbm, pos_hbm, loss_ref, dq_ref, dp_ref,
             q, pos, allp, qin, s, w, w_in, own, lse_own, lse_in,
             load_sem, p_send, p_recv, q_send, q_recv, l_send, l_recv):
    rows, width = q.shape
    n = rows // TILE
    dp, me = lax.axis_index("dp"), lax.axis_index("neg")
    peers = [(dp, jnp.bitwise_xor(me, stride)) for stride in strides]

    loads = [
        pltpu.make_async_copy(p_hbm, allp.at[pl.ds(0, rows)], load_sem.at[0]),
        pltpu.make_async_copy(q_hbm, q, load_sem.at[1]),
        pltpu.make_async_copy(pos_hbm, pos, load_sem.at[2]),
    ]
    for load in loads:
        load.start()
    barrier = pltpu.get_barrier_semaphore()
    for peer in peers:
        pl.semaphore_signal(barrier, inc=1, device_id=peer, device_id_type=MESH)
    pl.semaphore_wait(barrier, len(peers))

    def tile_of(c):
        return pl.ds(pl.multiple_of(c * TILE, TILE), TILE)

    def send_p(i):
        return pltpu.make_async_remote_copy(
            src_ref=p_hbm, dst_ref=allp.at[pl.ds((i + 1) * rows, rows)],
            send_sem=p_send.at[i], recv_sem=p_recv.at[i], device_id=peers[i], device_id_type=MESH)

    def send_q(i, c):
        return pltpu.make_async_remote_copy(
            src_ref=q_hbm.at[tile_of(c)], dst_ref=qin.at[c, pl.ds(i * TILE, TILE)],
            send_sem=q_send.at[i, c], recv_sem=q_recv.at[i, c], device_id=peers[i], device_id_type=MESH)

    def send_lse(i):
        return pltpu.make_async_remote_copy(
            src_ref=lse_own, dst_ref=lse_in.at[i], send_sem=l_send.at[i], recv_sem=l_recv.at[i],
            device_id=peers[i], device_id_type=MESH)

    for i in (0, 1):
        send_p(i).start()
    for c in range(EARLY):
        for i in (0, 1):
            send_q(i, c).start()
    for load in loads:
        load.wait()

    def fold(tile, combine):
        return combine(tile.reshape(TILE // 8, 8, rows), axis=0)

    def scores(c, top):
        tile = nt(allp[tile_of(c)], q[...]) * scale
        s[tile_of(c)] = tile
        return jnp.maximum(top, fold(tile, jnp.max))

    def arrived_scores(c, top):
        for i in (0, 1):
            @pl.when(c == (i + 1) * n)
            def _():
                send_p(i).wait_recv()
        return scores(c, top)

    top = lax.fori_loop(0, 3 * n, arrived_scores, jnp.full((8, rows), -jnp.inf, jnp.float32))
    top = jnp.max(top, axis=0, keepdims=True)

    def add_up(c, total):
        return total + fold(jnp.exp(s[tile_of(c)] - top), jnp.sum)

    total = lax.fori_loop(0, 3 * n, add_up, jnp.zeros((8, rows), jnp.float32))
    lse = top + jnp.log(jnp.sum(total, axis=0, keepdims=True))
    lse_own[...] = jnp.broadcast_to(lse, lse_own.shape)
    for i in (0, 1):
        send_lse(i).start()
    for c in range(EARLY, n):
        for i in (0, 1):
            send_q(i, c).start()

    positive = pos[...]

    def weigh_own(c, picked):
        tile = s[tile_of(c)]
        hit = lax.broadcasted_iota(jnp.int32, tile.shape, 0) + c * TILE == positive
        w[tile_of(c)] = (jnp.exp(tile - lse) - hit.astype(jnp.float32)).astype(jnp.bfloat16)
        return picked + fold(jnp.where(hit, tile, 0.0), jnp.sum)

    def weigh(c, _):
        w[tile_of(c)] = jnp.exp(s[tile_of(c)] - lse).astype(jnp.bfloat16)
        return 0

    picked = lax.fori_loop(0, n, weigh_own, jnp.zeros((8, rows), jnp.float32))
    loss_ref[...] = lse - jnp.sum(picked, axis=0, keepdims=True)
    lax.fori_loop(n, 3 * n, weigh, 0)

    def local_grads(c, _):
        dq_ref[tile_of(c)] = tn(w[:, tile_of(c)], allp[...]).astype(jnp.bfloat16)
        own[tile_of(c)] = nn(w[tile_of(c)], q[...])
        return 0

    lax.fori_loop(0, n, local_grads, 0)
    for i in (0, 1):
        send_lse(i).wait_recv()

    def arrived(c, _):
        for i in (0, 1):
            send_q(i, c).wait_recv()
        lses = jnp.concatenate([lse_in[i, 0:1, tile_of(c)] for i in (0, 1)], axis=1)
        tile = nt(allp[0:rows], qin[c]) * scale
        w_in[...] = jnp.exp(tile - lses).astype(jnp.bfloat16)

        def add(j, _):
            span = pl.ds(pl.multiple_of(j * FIN, FIN), FIN)
            total = own[span] + nn(w_in[span], qin[c])
            own[span] = total
            dp_ref[span] = total.astype(jnp.bfloat16)
            return 0

        lax.fori_loop(0, rows // FIN, add, 0)
        return 0

    lax.fori_loop(0, n, arrived, 0)

    for i in (0, 1):
        send_p(i).wait_send()
        send_lse(i).wait_send()
        for c in range(n):
            send_q(i, c).wait_send()


def call_exchange(level, half, scale, queries, passages, positives):
    rows, width = queries.shape
    n = rows // TILE
    vmem, dma = pltpu.VMEM, pltpu.SemaphoreType.DMA
    f32, bf16 = jnp.float32, jnp.bfloat16
    outside = pl.BlockSpec(memory_space=pltpu.HBM)
    inside = pl.BlockSpec(memory_space=pltpu.VMEM)
    return pl.pallas_call(
        functools.partial(exchange, (half, 2**level), scale),
        out_shape=(vmem((1, rows), f32), vmem((rows, width), bf16), vmem((rows, width), bf16)),
        in_specs=[outside] * 3,
        out_specs=(inside,) * 3,
        scratch_shapes=[
            vmem((rows, width), bf16),
            vmem((1, rows), jnp.int32),
            vmem((3 * rows, width), bf16),
            vmem((n, 2 * TILE, width), bf16),
            vmem((3 * rows, rows), f32),
            vmem((3 * rows, rows), bf16),
            vmem((rows, 2 * TILE), bf16),
            vmem((rows, width), f32),
            vmem((8, rows), f32),
            vmem((2, 8, rows), f32),
            dma((3,)),
            dma((2,)),
            dma((2,)),
            dma((2, n)),
            dma((2, n)),
            dma((2,)),
            dma((2,)),
        ],
        name=f"exchange_{level}",
        cost_estimate=pl.CostEstimate(
            flops=22 * rows * rows * width, bytes_accessed=8 * rows * width, transcendentals=8 * rows * rows),
        compiler_params=pltpu.CompilerParams(
            collective_id=level, has_side_effects=True, vmem_limit_bytes=32 * 2**20),
    )(queries, passages, positives)


def write_out(loss, dq, dp, loss_hbm, dq_hbm, dp_hbm, sem):
    n = dq.shape[0] // TILE
    copies = [pltpu.make_async_copy(loss, loss_hbm, sem.at[2 * n])]
    for c in range(n):
        block = pl.ds(c * TILE, TILE)
        copies.append(pltpu.make_async_copy(dq.at[block], dq_hbm.at[block], sem.at[c]))
        copies.append(pltpu.make_async_copy(dp.at[block], dp_hbm.at[block], sem.at[n + c]))
    for copy in copies:
        copy.start()
    for copy in copies:
        copy.wait()


def call_write_out(*parts):
    outside = pl.BlockSpec(memory_space=pltpu.HBM)
    inside = pl.BlockSpec(memory_space=pltpu.VMEM)
    return pl.pallas_call(
        write_out,
        out_shape=tuple(jax.ShapeDtypeStruct(part.shape, part.dtype) for part in parts),
        in_specs=[inside] * 3,
        out_specs=(outside,) * 3,
        scratch_shapes=[pltpu.SemaphoreType.DMA((2 * (parts[1].shape[0] // TILE) + 1,))],
        name="write_out",
        compiler_params=pltpu.CompilerParams(vmem_limit_bytes=8 * 2**20),
    )(*parts)


def choose(half, levels, partners, index):
    other = partners[0, 0] ^ partners[1, 0] ^ half
    place = jnp.int32(0)
    for j in range(1, levels):
        place = place + (other >= 2**j).astype(jnp.int32)
    index[0] = place


def call_choose(half, levels, partners):
    return pl.pallas_call(
        functools.partial(choose, half, levels),
        out_shape=pltpu.SMEM((1,), jnp.int32),
        in_specs=[pl.BlockSpec(memory_space=pltpu.SMEM)],
        out_specs=pl.BlockSpec(memory_space=pltpu.SMEM),
        name="choose",
    )(partners)


def per_device(queries, passages, partners, positives):
    rows, width = queries.shape
    half = lax.axis_size("neg") // 2
    levels = half.bit_length() - 1
    index = call_choose(half, levels, partners)[0]
    branches = [functools.partial(call_exchange, level, half, width ** (-0.5)) for level in range(levels)]
    parts = lax.switch(index, branches, queries, passages, positives.reshape(1, rows))
    loss, grad_queries, grad_passages = call_write_out(*parts)
    return loss.reshape(rows), grad_queries, grad_passages


def solution(mesh):
    placed = (P(("dp", "neg"), None), P(("dp", "neg"), None), P(), P(("dp", "neg")))
    return jax.shard_map(
        per_device,
        mesh=mesh,
        in_specs=placed,
        out_specs=(P(("dp", "neg")), P(("dp", "neg"), None), P(("dp", "neg"), None)),
        check_vma=False,
    )
```

```python
import functools

import jax
import jax.numpy as jnp
from jax import lax
from jax.experimental import pallas as pl
from jax.experimental.pallas import tpu as pltpu
from jax.sharding import PartitionSpec as P

MESH = pl.DeviceIdType.MESH
TILE = 128
EARLY = 2
FIN = 256


def nt(left, right):
    return lax.dot_general(left, right, (((1,), (1,)), ((), ())), preferred_element_type=jnp.float32)


def tn(left, right):
    return lax.dot_general(left, right, (((0,), (0,)), ((), ())), preferred_element_type=jnp.float32)


def nn(left, right):
    return jnp.dot(left, right, preferred_element_type=jnp.float32)


def exchange(strides, scale, q_hbm, p_hbm, pos_hbm, loss_ref, dq_ref, dp_ref,
             q, pos, allp, qin, s, w, w_in, own, lse_own, lse_in,
             load_sem, p_send, p_recv, q_send, q_recv, l_send, l_recv):
    rows, width = q.shape
    n = rows // TILE
    dp, me = lax.axis_index("dp"), lax.axis_index("neg")
    peers = [(dp, jnp.bitwise_xor(me, stride)) for stride in strides]

    loads = [
        pltpu.make_async_copy(p_hbm, allp.at[pl.ds(0, rows)], load_sem.at[0]),
        pltpu.make_async_copy(q_hbm, q, load_sem.at[1]),
        pltpu.make_async_copy(pos_hbm, pos, load_sem.at[2]),
    ]
    for load in loads:
        load.start()
    barrier = pltpu.get_barrier_semaphore()
    for peer in peers:
        pl.semaphore_signal(barrier, inc=1, device_id=peer, device_id_type=MESH)
    pl.semaphore_wait(barrier, len(peers))

    def tile_of(c):
        return pl.ds(pl.multiple_of(c * TILE, TILE), TILE)

    def send_p(i):
        return pltpu.make_async_remote_copy(
            src_ref=p_hbm, dst_ref=allp.at[pl.ds((i + 1) * rows, rows)],
            send_sem=p_send.at[i], recv_sem=p_recv.at[i], device_id=peers[i], device_id_type=MESH)

    def send_q(i, c):
        return pltpu.make_async_remote_copy(
            src_ref=q_hbm.at[tile_of(c)], dst_ref=qin.at[c, pl.ds(i * TILE, TILE)],
            send_sem=q_send.at[i, c], recv_sem=q_recv.at[i, c], device_id=peers[i], device_id_type=MESH)

    def send_lse(i):
        return pltpu.make_async_remote_copy(
            src_ref=lse_own, dst_ref=lse_in.at[i], send_sem=l_send.at[i], recv_sem=l_recv.at[i],
            device_id=peers[i], device_id_type=MESH)

    for i in (0, 1):
        send_p(i).start()
    for c in range(EARLY):
        for i in (0, 1):
            send_q(i, c).start()
    for load in loads:
        load.wait()

    def fold(tile, combine):
        return combine(tile.reshape(TILE // 8, 8, rows), axis=0)

    def scores(c, top):
        tile = nt(allp[tile_of(c)], q[...]) * scale
        s[tile_of(c)] = tile
        return jnp.maximum(top, fold(tile, jnp.max))

    def arrived_scores(c, top):
        for i in (0, 1):
            @pl.when(c == (i + 1) * n)
            def _():
                send_p(i).wait_recv()
        return scores(c, top)

    top = lax.fori_loop(0, 3 * n, arrived_scores, jnp.full((8, rows), -jnp.inf, jnp.float32))
    top = jnp.max(top, axis=0, keepdims=True)

    def add_up(c, total):
        return total + fold(jnp.exp(s[tile_of(c)] - top), jnp.sum)

    total = lax.fori_loop(0, 3 * n, add_up, jnp.zeros((8, rows), jnp.float32))
    lse = top + jnp.log(jnp.sum(total, axis=0, keepdims=True))
    lse_own[...] = jnp.broadcast_to(lse, lse_own.shape)
    for i in (0, 1):
        send_lse(i).start()
    for c in range(EARLY, n):
        for i in (0, 1):
            send_q(i, c).start()

    positive = pos[...]

    def weigh_own(c, picked):
        tile = s[tile_of(c)]
        hit = lax.broadcasted_iota(jnp.int32, tile.shape, 0) + c * TILE == positive
        w[tile_of(c)] = (jnp.exp(tile - lse) - hit.astype(jnp.float32)).astype(jnp.bfloat16)
        return picked + fold(jnp.where(hit, tile, 0.0), jnp.sum)

    def weigh(c, _):
        w[tile_of(c)] = jnp.exp(s[tile_of(c)] - lse).astype(jnp.bfloat16)
        return 0

    picked = lax.fori_loop(0, n, weigh_own, jnp.zeros((8, rows), jnp.float32))
    loss_ref[...] = lse - jnp.sum(picked, axis=0, keepdims=True)
    lax.fori_loop(n, 3 * n, weigh, 0)

    def local_grads(c, _):
        dq_ref[tile_of(c)] = tn(w[:, tile_of(c)], allp[...]).astype(jnp.bfloat16)
        own[tile_of(c)] = nn(w[tile_of(c)], q[...])
        return 0

    lax.fori_loop(0, n, local_grads, 0)
    for i in (0, 1):
        send_lse(i).wait_recv()

    def arrived(c, _):
        for i in (0, 1):
            send_q(i, c).wait_recv()
        lses = jnp.concatenate([lse_in[i, 0:1, tile_of(c)] for i in (0, 1)], axis=1)
        tile = nt(allp[0:rows], qin[c]) * scale
        w_in[...] = jnp.exp(tile - lses).astype(jnp.bfloat16)

        def add(j, _):
            span = pl.ds(pl.multiple_of(j * FIN, FIN), FIN)
            total = own[span] + nn(w_in[span], qin[c])
            own[span] = total
            dp_ref[span] = total.astype(jnp.bfloat16)
            return 0

        lax.fori_loop(0, rows // FIN, add, 0)
        return 0

    lax.fori_loop(0, n, arrived, 0)

    for i in (0, 1):
        send_p(i).wait_send()
        send_lse(i).wait_send()
        for c in range(n):
            send_q(i, c).wait_send()


def call_exchange(level, half, scale, queries, passages, positives):
    rows, width = queries.shape
    n = rows // TILE
    vmem, dma = pltpu.VMEM, pltpu.SemaphoreType.DMA
    f32, bf16 = jnp.float32, jnp.bfloat16
    outside = pl.BlockSpec(memory_space=pltpu.HBM)
    inside = pl.BlockSpec(memory_space=pltpu.VMEM)
    return pl.pallas_call(
        functools.partial(exchange, (half, 2**level), scale),
        out_shape=(vmem((1, rows), f32), vmem((rows, width), bf16), vmem((rows, width), bf16)),
        in_specs=[outside] * 3,
        out_specs=(inside,) * 3,
        scratch_shapes=[
            vmem((rows, width), bf16),
            vmem((1, rows), jnp.int32),
            vmem((3 * rows, width), bf16),
            vmem((n, 2 * TILE, width), bf16),
            vmem((3 * rows, rows), f32),
            vmem((3 * rows, rows), bf16),
            vmem((rows, 2 * TILE), bf16),
            vmem((rows, width), f32),
            vmem((8, rows), f32),
            vmem((2, 8, rows), f32),
            dma((3,)),
            dma((2,)),
            dma((2,)),
            dma((2, n)),
            dma((2, n)),
            dma((2,)),
            dma((2,)),
        ],
        name=f"exchange_{level}",
        cost_estimate=pl.CostEstimate(
            flops=22 * rows * rows * width, bytes_accessed=8 * rows * width, transcendentals=8 * rows * rows),
        compiler_params=pltpu.CompilerParams(
            collective_id=level, has_side_effects=True, vmem_limit_bytes=32 * 2**20),
    )(*[pltpu.with_memory_space_constraint(x, pltpu.HBM) for x in (queries, passages, positives)])


def write_out(loss, dq, dp, loss_hbm, dq_hbm, dp_hbm, sem):
    n = dq.shape[0] // TILE
    copies = [pltpu.make_async_copy(loss, loss_hbm, sem.at[2 * n])]
    for c in range(n):
        block = pl.ds(c * TILE, TILE)
        copies.append(pltpu.make_async_copy(dq.at[block], dq_hbm.at[block], sem.at[c]))
        copies.append(pltpu.make_async_copy(dp.at[block], dp_hbm.at[block], sem.at[n + c]))
    for copy in copies:
        copy.start()
    for copy in copies:
        copy.wait()


def call_write_out(*parts):
    outside = pl.BlockSpec(memory_space=pltpu.HBM)
    inside = pl.BlockSpec(memory_space=pltpu.VMEM)
    return pl.pallas_call(
        write_out,
        out_shape=tuple(jax.ShapeDtypeStruct(part.shape, part.dtype) for part in parts),
        in_specs=[inside] * 3,
        out_specs=(outside,) * 3,
        scratch_shapes=[pltpu.SemaphoreType.DMA((2 * (parts[1].shape[0] // TILE) + 1,))],
        name="write_out",
        compiler_params=pltpu.CompilerParams(vmem_limit_bytes=8 * 2**20),
    )(*parts)


def choose(half, levels, partners, index):
    other = partners[0, 0] ^ partners[1, 0] ^ half
    place = jnp.int32(0)
    for j in range(1, levels):
        place = place + (other >= 2**j).astype(jnp.int32)
    index[0] = place


def call_choose(half, levels, partners):
    return pl.pallas_call(
        functools.partial(choose, half, levels),
        out_shape=pltpu.SMEM((1,), jnp.int32),
        in_specs=[pl.BlockSpec(memory_space=pltpu.SMEM)],
        out_specs=pl.BlockSpec(memory_space=pltpu.SMEM),
        name="choose",
    )(partners)


def per_device(queries, passages, partners, positives):
    rows, width = queries.shape
    half = lax.axis_size("neg") // 2
    levels = half.bit_length() - 1
    index = call_choose(half, levels, partners)[0]
    branches = [functools.partial(call_exchange, level, half, width ** (-0.5)) for level in range(levels)]
    parts = lax.switch(index, branches, queries, passages, positives.reshape(1, rows))
    loss, grad_queries, grad_passages = call_write_out(*parts)
    return loss.reshape(rows), grad_queries, grad_passages


def solution(mesh):
    placed = (P(("dp", "neg"), None), P(("dp", "neg"), None), P(), P(("dp", "neg")))
    return jax.shard_map(
        per_device,
        mesh=mesh,
        in_specs=placed,
        out_specs=(P(("dp", "neg")), P(("dp", "neg"), None), P(("dp", "neg"), None)),
        check_vma=False,
    )
```

```python
import functools

import jax
import jax.numpy as jnp
from jax import lax
from jax.experimental import pallas as pl
from jax.experimental.pallas import tpu as pltpu
from jax.sharding import PartitionSpec as P

MESH = pl.DeviceIdType.MESH
TILE = 128
EARLY = 2
HALF = 256


def nt(left, right):
    return lax.dot_general(left, right, (((1,), (1,)), ((), ())), preferred_element_type=jnp.float32)


def tn(left, right):
    return lax.dot_general(left, right, (((0,), (0,)), ((), ())), preferred_element_type=jnp.float32)


def nn(left, right):
    return jnp.dot(left, right, preferred_element_type=jnp.float32)


def exchange(strides, scale, q_hbm, p_hbm, pos_hbm, loss_ref, dq_ref, dp_ref,
             q, pos, allp, qin, s, w, w_in, own, lse_own, lse_in,
             load_sem, p_send, p_recv, q_send, q_recv, l_send, l_recv):
    rows, width = q.shape
    n = rows // TILE
    dp, me = lax.axis_index("dp"), lax.axis_index("neg")
    peers = [(dp, jnp.bitwise_xor(me, stride)) for stride in strides]

    loads = [
        pltpu.make_async_copy(p_hbm, allp.at[pl.ds(0, rows)], load_sem.at[0]),
        pltpu.make_async_copy(q_hbm, q, load_sem.at[1]),
        pltpu.make_async_copy(pos_hbm, pos, load_sem.at[2]),
    ]
    for load in loads:
        load.start()
    barrier = pltpu.get_barrier_semaphore()
    for peer in peers:
        pl.semaphore_signal(barrier, inc=1, device_id=peer, device_id_type=MESH)
    pl.semaphore_wait(barrier, len(peers))

    def tile_of(c):
        return pl.ds(pl.multiple_of(c * TILE, TILE), TILE)

    def send_p(i):
        return pltpu.make_async_remote_copy(
            src_ref=p_hbm, dst_ref=allp.at[pl.ds((i + 1) * rows, rows)],
            send_sem=p_send.at[i], recv_sem=p_recv.at[i], device_id=peers[i], device_id_type=MESH)

    def send_q(i, c):
        return pltpu.make_async_remote_copy(
            src_ref=q_hbm.at[tile_of(c)], dst_ref=qin.at[c, pl.ds(i * TILE, TILE)],
            send_sem=q_send.at[i, c], recv_sem=q_recv.at[i, c], device_id=peers[i], device_id_type=MESH)

    def send_lse(i):
        return pltpu.make_async_remote_copy(
            src_ref=lse_own, dst_ref=lse_in.at[i], send_sem=l_send.at[i], recv_sem=l_recv.at[i],
            device_id=peers[i], device_id_type=MESH)

    for i in (0, 1):
        send_p(i).start()
    for c in range(EARLY):
        for i in (0, 1):
            send_q(i, c).start()
    for load in loads:
        load.wait()

    def fold(tile, combine):
        return combine(tile.reshape(TILE // 8, 8, rows), axis=0)

    def scores(c, top):
        tile = nt(allp[tile_of(c)], q[...]) * scale
        s[tile_of(c)] = tile
        return jnp.maximum(top, fold(tile, jnp.max))

    def arrived_scores(c, top):
        for i in (0, 1):
            @pl.when(c == (i + 1) * n)
            def _():
                send_p(i).wait_recv()
        return scores(c, top)

    top = lax.fori_loop(0, 3 * n, arrived_scores, jnp.full((8, rows), -jnp.inf, jnp.float32))
    top = jnp.max(top, axis=0, keepdims=True)

    def add_up(c, total):
        return total + fold(jnp.exp(s[tile_of(c)] - top), jnp.sum)

    total = lax.fori_loop(0, 3 * n, add_up, jnp.zeros((8, rows), jnp.float32))
    lse = top + jnp.log(jnp.sum(total, axis=0, keepdims=True))
    lse_own[...] = jnp.broadcast_to(lse, lse_own.shape)
    for i in (0, 1):
        send_lse(i).start()
    for c in range(EARLY, n):
        for i in (0, 1):
            send_q(i, c).start()

    positive = pos[...]

    def weigh_own(c, picked):
        tile = s[tile_of(c)]
        hit = lax.broadcasted_iota(jnp.int32, tile.shape, 0) + c * TILE == positive
        w[tile_of(c)] = (jnp.exp(tile - lse) - hit.astype(jnp.float32)).astype(jnp.bfloat16)
        return picked + fold(jnp.where(hit, tile, 0.0), jnp.sum)

    def weigh(c, _):
        w[tile_of(c)] = jnp.exp(s[tile_of(c)] - lse).astype(jnp.bfloat16)
        return 0

    picked = lax.fori_loop(0, n, weigh_own, jnp.zeros((8, rows), jnp.float32))
    loss_ref[...] = lse - jnp.sum(picked, axis=0, keepdims=True)
    lax.fori_loop(n, 3 * n, weigh, 0)

    def local_grads(c, _):
        dq_ref[tile_of(c)] = tn(w[:, tile_of(c)], allp[...]).astype(jnp.bfloat16)
        own[tile_of(c)] = nn(w[tile_of(c)], q[...])
        return 0

    lax.fori_loop(0, n, local_grads, 0)
    for i in (0, 1):
        send_lse(i).wait_recv()

    spans = [slice(j * HALF, (j + 1) * HALF) for j in range(rows // HALF)]

    def arrived(c, _):
        for i in (0, 1):
            send_q(i, c).wait_recv()
        lses = jnp.concatenate([lse_in[i, 0:1, tile_of(c)] for i in (0, 1)], axis=1)
        for span in spans:
            tile = nt(allp[span], qin[c]) * scale
            w_in[span] = jnp.exp(tile - lses).astype(jnp.bfloat16)
        for span in spans:
            total = own[span] + nn(w_in[span], qin[c])
            own[span] = total
            dp_ref[span] = total.astype(jnp.bfloat16)
        return 0

    lax.fori_loop(0, n, arrived, 0)

    for i in (0, 1):
        send_p(i).wait_send()
        send_lse(i).wait_send()
        for c in range(n):
            send_q(i, c).wait_send()


def call_exchange(level, half, scale, queries, passages, positives):
    rows, width = queries.shape
    n = rows // TILE
    vmem, dma = pltpu.VMEM, pltpu.SemaphoreType.DMA
    f32, bf16 = jnp.float32, jnp.bfloat16
    outside = pl.BlockSpec(memory_space=pltpu.HBM)
    inside = pl.BlockSpec(memory_space=pltpu.VMEM)
    return pl.pallas_call(
        functools.partial(exchange, (half, 2**level), scale),
        out_shape=(vmem((1, rows), f32), vmem((rows, width), bf16), vmem((rows, width), bf16)),
        in_specs=[outside] * 3,
        out_specs=(inside,) * 3,
        scratch_shapes=[
            vmem((rows, width), bf16),
            vmem((1, rows), jnp.int32),
            vmem((3 * rows, width), bf16),
            vmem((n, 2 * TILE, width), bf16),
            vmem((3 * rows, rows), f32),
            vmem((3 * rows, rows), bf16),
            vmem((rows, 2 * TILE), bf16),
            vmem((rows, width), f32),
            vmem((8, rows), f32),
            vmem((2, 8, rows), f32),
            dma((3,)),
            dma((2,)),
            dma((2,)),
            dma((2, n)),
            dma((2, n)),
            dma((2,)),
            dma((2,)),
        ],
        name=f"exchange_{level}",
        cost_estimate=pl.CostEstimate(
            flops=22 * rows * rows * width, bytes_accessed=8 * rows * width, transcendentals=8 * rows * rows),
        compiler_params=pltpu.CompilerParams(
            collective_id=level, has_side_effects=True, vmem_limit_bytes=32 * 2**20),
    )(*[pltpu.with_memory_space_constraint(x, pltpu.HBM) for x in (queries, passages, positives)])


def write_out(loss, dq, dp, loss_hbm, dq_hbm, dp_hbm, sem):
    n = dq.shape[0] // TILE
    copies = [pltpu.make_async_copy(loss, loss_hbm, sem.at[2 * n])]
    for c in range(n):
        block = pl.ds(c * TILE, TILE)
        copies.append(pltpu.make_async_copy(dq.at[block], dq_hbm.at[block], sem.at[c]))
        copies.append(pltpu.make_async_copy(dp.at[block], dp_hbm.at[block], sem.at[n + c]))
    for copy in copies:
        copy.start()
    for copy in copies:
        copy.wait()


def call_write_out(*parts):
    outside = pl.BlockSpec(memory_space=pltpu.HBM)
    inside = pl.BlockSpec(memory_space=pltpu.VMEM)
    return pl.pallas_call(
        write_out,
        out_shape=tuple(jax.ShapeDtypeStruct(part.shape, part.dtype) for part in parts),
        in_specs=[inside] * 3,
        out_specs=(outside,) * 3,
        scratch_shapes=[pltpu.SemaphoreType.DMA((2 * (parts[1].shape[0] // TILE) + 1,))],
        name="write_out",
        compiler_params=pltpu.CompilerParams(vmem_limit_bytes=8 * 2**20),
    )(*parts)


def choose(half, levels, partners, index):
    other = partners[0, 0] ^ partners[1, 0] ^ half
    place = jnp.int32(0)
    for j in range(1, levels):
        place = place + (other >= 2**j).astype(jnp.int32)
    index[0] = place


def call_choose(half, levels, partners):
    return pl.pallas_call(
        functools.partial(choose, half, levels),
        out_shape=pltpu.SMEM((1,), jnp.int32),
        in_specs=[pl.BlockSpec(memory_space=pltpu.SMEM)],
        out_specs=pl.BlockSpec(memory_space=pltpu.SMEM),
        name="choose",
    )(partners)


def per_device(queries, passages, partners, positives):
    rows, width = queries.shape
    half = lax.axis_size("neg") // 2
    levels = half.bit_length() - 1
    index = call_choose(half, levels, partners)[0]
    branches = [functools.partial(call_exchange, level, half, width ** (-0.5)) for level in range(levels)]
    parts = lax.switch(index, branches, queries, passages, positives.reshape(1, rows))
    loss, grad_queries, grad_passages = call_write_out(*parts)
    return loss.reshape(rows), grad_queries, grad_passages


def solution(mesh):
    placed = (P(("dp", "neg"), None), P(("dp", "neg"), None), P(), P(("dp", "neg")))
    return jax.shard_map(
        per_device,
        mesh=mesh,
        in_specs=placed,
        out_specs=(P(("dp", "neg")), P(("dp", "neg"), None), P(("dp", "neg"), None)),
        check_vma=False,
    )
```

```python
import functools

import jax
import jax.numpy as jnp
from jax import lax
from jax.experimental import pallas as pl
from jax.experimental.pallas import tpu as pltpu
from jax.sharding import PartitionSpec as P

MESH = pl.DeviceIdType.MESH
TILE = 128
EARLY = 2
HALF = 256


def nt(left, right):
    return lax.dot_general(left, right, (((1,), (1,)), ((), ())), preferred_element_type=jnp.float32)


def tn(left, right):
    return lax.dot_general(left, right, (((0,), (0,)), ((), ())), preferred_element_type=jnp.float32)


def nn(left, right):
    return jnp.dot(left, right, preferred_element_type=jnp.float32)


def exchange(strides, scale, q_hbm, p_hbm, pos_hbm, loss_ref, dq_ref, dp_ref,
             q, pos, allp, qin, s, w, w_in, own, lse_own, lse_in,
             load_sem, p_send, p_recv, q_send, q_recv, l_send, l_recv):
    rows, width = q.shape
    n = rows // TILE
    dp, me = lax.axis_index("dp"), lax.axis_index("neg")
    peers = [(dp, jnp.bitwise_xor(me, stride)) for stride in strides]

    loads = [
        pltpu.make_async_copy(p_hbm, allp.at[pl.ds(0, rows)], load_sem.at[0]),
        pltpu.make_async_copy(q_hbm, q, load_sem.at[1]),
        pltpu.make_async_copy(pos_hbm, pos, load_sem.at[2]),
    ]
    barrier = pltpu.get_barrier_semaphore()
    for peer in peers:
        pl.semaphore_signal(barrier, inc=1, device_id=peer, device_id_type=MESH)
    pl.semaphore_wait(barrier, len(peers))

    def tile_of(c):
        return pl.ds(pl.multiple_of(c * TILE, TILE), TILE)

    def send_p(i):
        return pltpu.make_async_remote_copy(
            src_ref=p_hbm, dst_ref=allp.at[pl.ds((i + 1) * rows, rows)],
            send_sem=p_send.at[i], recv_sem=p_recv.at[i], device_id=peers[i], device_id_type=MESH)

    def send_q(i, c):
        return pltpu.make_async_remote_copy(
            src_ref=q_hbm.at[tile_of(c)], dst_ref=qin.at[c, pl.ds(i * TILE, TILE)],
            send_sem=q_send.at[i, c], recv_sem=q_recv.at[i, c], device_id=peers[i], device_id_type=MESH)

    def send_lse(i):
        return pltpu.make_async_remote_copy(
            src_ref=lse_own, dst_ref=lse_in.at[i], send_sem=l_send.at[i], recv_sem=l_recv.at[i],
            device_id=peers[i], device_id_type=MESH)

    for i in (0, 1):
        send_p(i).start()
    for load in loads:
        load.start()
    for c in range(EARLY):
        for i in (0, 1):
            send_q(i, c).start()
    for load in loads:
        load.wait()

    def fold(tile, combine):
        return combine(tile.reshape(TILE // 8, 8, rows), axis=0)

    def scores(c, top):
        tile = nt(allp[tile_of(c)], q[...]) * scale
        s[tile_of(c)] = tile
        return jnp.maximum(top, fold(tile, jnp.max))

    def arrived_scores(c, top):
        for i in (0, 1):
            @pl.when(c == (i + 1) * n)
            def _():
                send_p(i).wait_recv()
        return scores(c, top)

    top = lax.fori_loop(0, 3 * n, arrived_scores, jnp.full((8, rows), -jnp.inf, jnp.float32))
    top = jnp.max(top, axis=0, keepdims=True)

    def add_up(c, total):
        return total + fold(jnp.exp(s[tile_of(c)] - top), jnp.sum)

    total = lax.fori_loop(0, 3 * n, add_up, jnp.zeros((8, rows), jnp.float32))
    lse = top + jnp.log(jnp.sum(total, axis=0, keepdims=True))
    lse_own[...] = jnp.broadcast_to(lse, lse_own.shape)
    for i in (0, 1):
        send_lse(i).start()
    for c in range(EARLY, n):
        for i in (0, 1):
            send_q(i, c).start()

    positive = pos[...]

    def weigh_own(c, picked):
        tile = s[tile_of(c)]
        hit = lax.broadcasted_iota(jnp.int32, tile.shape, 0) + c * TILE == positive
        w[tile_of(c)] = (jnp.exp(tile - lse) - hit.astype(jnp.float32)).astype(jnp.bfloat16)
        return picked + fold(jnp.where(hit, tile, 0.0), jnp.sum)

    def weigh(c, _):
        w[tile_of(c)] = jnp.exp(s[tile_of(c)] - lse).astype(jnp.bfloat16)
        return 0

    picked = lax.fori_loop(0, n, weigh_own, jnp.zeros((8, rows), jnp.float32))
    loss_ref[...] = lse - jnp.sum(picked, axis=0, keepdims=True)
    lax.fori_loop(n, 3 * n, weigh, 0)

    def local_grads(c, _):
        dq_ref[tile_of(c)] = tn(w[:, tile_of(c)], allp[...]).astype(jnp.bfloat16)
        own[tile_of(c)] = nn(w[tile_of(c)], q[...])
        return 0

    lax.fori_loop(0, n, local_grads, 0)
    for i in (0, 1):
        send_lse(i).wait_recv()

    spans = [slice(j * HALF, (j + 1) * HALF) for j in range(rows // HALF)]

    def arrived(c, _):
        for i in (0, 1):
            send_q(i, c).wait_recv()
        lses = jnp.concatenate([lse_in[i, 0:1, tile_of(c)] for i in (0, 1)], axis=1)
        for span in spans:
            tile = nt(allp[span], qin[c]) * scale
            w_in[span] = jnp.exp(tile - lses).astype(jnp.bfloat16)
        for span in spans:
            total = own[span] + nn(w_in[span], qin[c])
            own[span] = total
            dp_ref[span] = total.astype(jnp.bfloat16)
        return 0

    lax.fori_loop(0, n, arrived, 0)

    for i in (0, 1):
        send_p(i).wait_send()
        send_lse(i).wait_send()
        for c in range(n):
            send_q(i, c).wait_send()


def call_exchange(level, half, scale, queries, passages, positives):
    rows, width = queries.shape
    n = rows // TILE
    vmem, dma = pltpu.VMEM, pltpu.SemaphoreType.DMA
    f32, bf16 = jnp.float32, jnp.bfloat16
    outside = pl.BlockSpec(memory_space=pltpu.HBM)
    inside = pl.BlockSpec(memory_space=pltpu.VMEM)
    return pl.pallas_call(
        functools.partial(exchange, (half, 2**level), scale),
        out_shape=(vmem((1, rows), f32), vmem((rows, width), bf16), vmem((rows, width), bf16)),
        in_specs=[outside] * 3,
        out_specs=(inside,) * 3,
        scratch_shapes=[
            vmem((rows, width), bf16),
            vmem((1, rows), jnp.int32),
            vmem((3 * rows, width), bf16),
            vmem((n, 2 * TILE, width), bf16),
            vmem((3 * rows, rows), f32),
            vmem((3 * rows, rows), bf16),
            vmem((rows, 2 * TILE), bf16),
            vmem((rows, width), f32),
            vmem((8, rows), f32),
            vmem((2, 8, rows), f32),
            dma((3,)),
            dma((2,)),
            dma((2,)),
            dma((2, n)),
            dma((2, n)),
            dma((2,)),
            dma((2,)),
        ],
        name=f"exchange_{level}",
        cost_estimate=pl.CostEstimate(
            flops=22 * rows * rows * width, bytes_accessed=8 * rows * width, transcendentals=8 * rows * rows),
        compiler_params=pltpu.CompilerParams(
            collective_id=level, has_side_effects=True, vmem_limit_bytes=32 * 2**20),
    )(*[pltpu.with_memory_space_constraint(x, pltpu.HBM) for x in (queries, passages, positives)])


def write_out(loss, dq, dp, loss_hbm, dq_hbm, dp_hbm, sem):
    n = dq.shape[0] // TILE
    copies = [pltpu.make_async_copy(loss, loss_hbm, sem.at[2 * n])]
    for c in range(n):
        block = pl.ds(c * TILE, TILE)
        copies.append(pltpu.make_async_copy(dq.at[block], dq_hbm.at[block], sem.at[c]))
        copies.append(pltpu.make_async_copy(dp.at[block], dp_hbm.at[block], sem.at[n + c]))
    for copy in copies:
        copy.start()
    for copy in copies:
        copy.wait()


def call_write_out(*parts):
    outside = pl.BlockSpec(memory_space=pltpu.HBM)
    inside = pl.BlockSpec(memory_space=pltpu.VMEM)
    return pl.pallas_call(
        write_out,
        out_shape=tuple(jax.ShapeDtypeStruct(part.shape, part.dtype) for part in parts),
        in_specs=[inside] * 3,
        out_specs=(outside,) * 3,
        scratch_shapes=[pltpu.SemaphoreType.DMA((2 * (parts[1].shape[0] // TILE) + 1,))],
        name="write_out",
        compiler_params=pltpu.CompilerParams(vmem_limit_bytes=8 * 2**20),
    )(*parts)


def choose(half, levels, partners, index):
    other = partners[0, 0] ^ partners[1, 0] ^ half
    place = jnp.int32(0)
    for j in range(1, levels):
        place = place + (other >= 2**j).astype(jnp.int32)
    index[0] = place


def call_choose(half, levels, partners):
    return pl.pallas_call(
        functools.partial(choose, half, levels),
        out_shape=pltpu.SMEM((1,), jnp.int32),
        in_specs=[pl.BlockSpec(memory_space=pltpu.SMEM)],
        out_specs=pl.BlockSpec(memory_space=pltpu.SMEM),
        name="choose",
    )(partners)


def per_device(queries, passages, partners, positives):
    rows, width = queries.shape
    half = lax.axis_size("neg") // 2
    levels = half.bit_length() - 1
    index = call_choose(half, levels, partners)[0]
    branches = [functools.partial(call_exchange, level, half, width ** (-0.5)) for level in range(levels)]
    parts = lax.switch(index, branches, queries, passages, positives.reshape(1, rows))
    loss, grad_queries, grad_passages = call_write_out(*parts)
    return loss.reshape(rows), grad_queries, grad_passages


def solution(mesh):
    placed = (P(("dp", "neg"), None), P(("dp", "neg"), None), P(), P(("dp", "neg")))
    return jax.shard_map(
        per_device,
        mesh=mesh,
        in_specs=placed,
        out_specs=(P(("dp", "neg")), P(("dp", "neg"), None), P(("dp", "neg"), None)),
        check_vma=False,
    )
```
